256 devices in a mesh: ctx: 32 (over z, y_lo, core), tp: 8 (over y_hi, x).
Axes of the slice: x: 4, y: 4 (y_hi: 2, y_lo: 2; y = y_hi * 2 + y_lo), z: 8, core: 2. Of those that a mesh axis runs over, the one named last changes fastest.
Arguments:
- previous_hidden: bfloat16 [16384, 4096], P('ctx', 'tp'), may hold values from -6 to 6
- output_weight: bfloat16 [4096, 4096], P('tp', 'ctx'), may hold values from -0.09375 to 0.09375
- adapter_down_weight: bfloat16 [4096, 128], P('tp'), may hold values from -0.09375 to 0.09375
- adapter_up_weight: bfloat16 [128, 4096], P('tp'), may hold values from -0.5 to 0.5
- stream: bfloat16 [16384, 4096], P(('ctx', 'tp')), may hold values from -6 to 6
- prenorm_gain: bfloat16 [4096], replicated, may hold values from 0.25 to 1.75
- input_weight: bfloat16 [3, 4096, 4096], P(None, 'ctx', 'tp'), may hold values from -0.09375 to 0.09375
- short_kernel: float32 [3, 7, 4096], P(None, None, 'tp'), may hold values from -2.5 to 2.5
- long_kernel: float32 [128, 4096], P(None, 'tp'), may hold values from -0.5 to 0.5
- long_direct_bias: float32 [4096], P('tp'), may hold values from -6 to 6
Outputs:
- new_stream: bfloat16 [16384, 4096], P(('ctx', 'tp'))
- mixer_out: bfloat16 [16384, 4096], P('ctx', 'tp')
The draws below stay inside these ranges and needn't reach their ends.
All inputs are finite; a program needn't handle non-finite values.
Results may differ from the reference program's by a relative error of at most 0.012.
Values may be sent and summed in bfloat16 or wider, within the bound.
No kernel may reach another device: no remote copies, remote signals or barrier semaphores. Data moves between devices by JAX's collectives and lax.ppermute only.
A program may use at most 128 MiB of HBM per device.

```python
import jax
import jax.numpy as jnp
from jax import lax

MODEL_WIDTH = 4096
HYENA_CHANNELS = 4096
ADAPTER_RANK = 128
SHORT = 7
LONG = 128
TOKENS = 16384


def levels(own_key, shape, shards, least, high):
    factor_of = 1.0
    for dim, parts in shards:
        steps = jax.random.uniform(jax.random.fold_in(jax.random.fold_in(own_key, 6), dim), (parts,), jnp.float32, least / len(shards), high / len(shards))
        factor_of = factor_of * jnp.repeat(jnp.exp(steps), shape[dim] // parts).reshape((-1,) + (1,) * (len(shape) - 1 - dim))
    return factor_of


def noise(stream_key, extent, scale, bound, pieces=(), dtype=jnp.bfloat16):
    factor_of = levels(stream_key, extent, pieces, -0.22, 0.18) if pieces else 1.0
    drawn = jax.random.normal(stream_key, extent, jnp.float32) * scale * factor_of
    return jnp.minimum(jnp.maximum(drawn, -bound), bound).astype(dtype)


def setup_inputs(seed: int = 0) -> dict:
    splits = jax.random.split(jax.random.key(seed), 11)
    previous_hidden = noise(splits[0], (TOKENS, HYENA_CHANNELS), 1.0, 6.0, ((0, 32), (1, 8)))
    output_weight = noise(splits[1], (HYENA_CHANNELS, MODEL_WIDTH), HYENA_CHANNELS ** -0.5, 0.09375, ((0, 8), (1, 32)))
    adapter_down_weight = noise(splits[2], (HYENA_CHANNELS, ADAPTER_RANK), HYENA_CHANNELS ** -0.5, 0.09375, ((0, 8),))
    adapter_up_weight = noise(splits[3], (ADAPTER_RANK, MODEL_WIDTH), ADAPTER_RANK ** -0.5, 0.5, ((0, 8),))
    stream = noise(splits[4], (TOKENS, MODEL_WIDTH), 1.0, 6.0, ((0, 256),))
    prenorm_gain = jnp.clip(1.0 + 0.15 * jax.random.normal(splits[5], (MODEL_WIDTH,), jnp.float32), 0.25, 1.75).astype(jnp.bfloat16)
    input_weight = noise(splits[6], (3, MODEL_WIDTH, HYENA_CHANNELS), MODEL_WIDTH ** -0.5, 0.09375, ((1, 32), (2, 8)))
    short_kernel = noise(splits[7], (3, SHORT, HYENA_CHANNELS), 0.4, 2.5, ((2, 8),), jnp.float32)
    long_kernel = noise(splits[8], (LONG, HYENA_CHANNELS), 0.09, 0.5, ((1, 8),), jnp.float32)
    long_direct_bias = noise(splits[9], (HYENA_CHANNELS,), 1.0, 6.0, ((0, 8),), jnp.float32)
    return {"previous_hidden": previous_hidden, "output_weight": output_weight, "adapter_down_weight": adapter_down_weight, "adapter_up_weight": adapter_up_weight, "stream": stream, "prenorm_gain": prenorm_gain, "input_weight": input_weight, "short_kernel": short_kernel, "long_kernel": long_kernel, "long_direct_bias": long_direct_bias}


adapter_scale = 0.5
norm_eps = 1e-05

def featurize(extended, filters):
    taps = filters.shape[1]
    length = extended.shape[1] - taps + 1
    running = jnp.zeros((extended.shape[0], length, extended.shape[2]), jnp.float32)
    for j in range(taps):
        running = running + filters[:, j, None, :] * extended[:, taps - 1 - j:taps - 1 - j + length, :].astype(jnp.float32)
    return running

def long_conv(extended, filters, bias_row):
    taps = filters.shape[0]
    length = extended.shape[0] - taps + 1
    running = bias_row[None, :] * extended[taps - 1:, :].astype(jnp.float32)
    for j in range(taps):
        running = running + filters[j][None, :] * extended[taps - 1 - j:taps - 1 - j + length, :].astype(jnp.float32)
    return running

def reference(previous_hidden, output_weight, adapter_down_weight, adapter_up_weight, stream, prenorm_gain, input_weight, short_kernel, long_kernel, long_direct_bias):
    base_term = jnp.dot(previous_hidden, output_weight, preferred_element_type=jnp.float32)
    reduced_rank = jnp.dot(previous_hidden, adapter_down_weight, preferred_element_type=jnp.float32)
    rank_adapter = jnp.dot(reduced_rank, adapter_up_weight.astype(jnp.float32), precision=lax.Precision.HIGHEST)
    partial_sum = base_term + adapter_scale * rank_adapter
    summed = stream.astype(jnp.float32) + partial_sum
    new_stream = summed.astype(jnp.bfloat16)
    scale_rows = lax.rsqrt(lax.optimization_barrier(jnp.mean(summed * summed, axis=1, keepdims=True)) + norm_eps)
    normed = (summed * scale_rows * prenorm_gain.astype(jnp.float32)[None, :]).astype(jnp.bfloat16)
    projected = jnp.stack([jnp.dot(normed, input_weight[b], preferred_element_type=jnp.float32) for b in range(3)]).astype(jnp.bfloat16)
    padded = jnp.pad(projected, ((0, 0), (SHORT - 1, 0), (0, 0)))
    featured = featurize(padded, short_kernel)
    inner_rows = (featured[1] * featured[2]).astype(jnp.bfloat16)
    convolved = long_conv(jnp.pad(inner_rows, ((LONG - 1, 0), (0, 0))), long_kernel, long_direct_bias)
    mixer_out = (featured[0] * convolved).astype(jnp.bfloat16)
    return (new_stream, mixer_out)
```

```python
import jax
import jax.numpy as jnp
import ml_dtypes
import numpy as np
from jax import lax
from jax.experimental import pallas as pl
from jax.experimental.pallas import tpu as pltpu
from jax.sharding import PartitionSpec as P

adapter_scale = 0.5
norm_eps = 1e-05
f32 = jnp.float32
bf16 = jnp.bfloat16

NZ, NX = 8, 4
ANY = pl.BlockSpec(memory_space=pl.ANY)
VMEM = pl.BlockSpec(memory_space=pltpu.VMEM)
SMEM = pl.BlockSpec(memory_space=pltpu.SMEM)


def joint(move):
    pairs = []
    for c in range(32):
        for t in range(8):
            z, q, y, x = c // 4, c % 4, t // 4, t % 4
            z2, q2, y2, x2 = move(z, q, y, x)
            pairs.append((c * 8 + t, (z2 * 4 + q2) * 8 + y2 * 4 + x2))
    return pairs


def sign(q):
    return 1 - 2 * (q % 2)


X_A = joint(lambda z, q, y, x: (z, q, y, (x + sign(q)) % NX))
X_B = joint(lambda z, q, y, x: (z, q, y, (x - sign(q)) % NX))
Y_HI = joint(lambda z, q, y, x: (z, q, 1 - y, x))
Z_A = joint(lambda z, q, y, x: ((z + sign(q)) % NZ, q, y, x))
Z_B = joint(lambda z, q, y, x: ((z - sign(q)) % NZ, q, y, x))
CORE = joint(lambda z, q, y, x: (z, q ^ 1, y, x))
Y_LO = joint(lambda z, q, y, x: (z, q ^ 2, y, x))
SWAP = joint(lambda z, q, y, x: (y * 4 + x, q, z // 4, z % 4))


def sent(value, pairs):
    return lax.ppermute(value, ("ctx", "tp"), pairs)


def gather_tp(own):
    a1 = sent(own, X_A)
    b1 = sent(own, X_B)
    y0 = sent(own, Y_HI)
    a2 = sent(a1, X_A)
    ya1 = sent(y0, X_A)
    yb1 = sent(y0, X_B)
    ya2 = sent(ya1, X_A)
    return [own, a1, a2, b1, y0, ya1, ya2, yb1]


def gather_z(own):
    a = [own]
    for _ in range(4):
        a.append(sent(a[-1], Z_A))
    b = [own]
    for _ in range(3):
        b.append(sent(b[-1], Z_B))
    return a + [b[3], b[2], b[1]]


def m1_kernel(idx, *refs):
    hid = refs[:8]
    own = refs[8:16]
    sib = refs[16:24]
    stream, out = refs[24:26]
    a_s, w_s, d_s, u_s, acc, sem_a, sem_w = refs[26:]
    core = idx[16]
    copies = []
    for i in range(8):
        copies.append(pltpu.make_async_copy(hid[i], a_s.at[i], sem_a.at[i]))
    for k in range(8):
        zk = idx[8 + k]
        for part, ref, c in ((0, own[k], core), (1, sib[(8 - k) % 8], 1 - core)):
            for ylo in range(2):
                n = (k * 2 + part) * 2 + ylo
                q = 2 * ylo + c
                copies.append(pltpu.make_async_copy(ref.at[ylo, pl.ds(0, 512)], w_s.at[k, q], sem_w.at[n, 0]))
                copies.append(pltpu.make_async_copy(ref.at[ylo, pl.ds(512, 128)], d_s.at[k, q], sem_w.at[n, 1]))
                copies.append(pltpu.make_async_copy(ref.at[ylo, pl.ds(640, 16)], u_s.at[zk, q], sem_w.at[n, 2]))
    for copy in copies:
        copy.start()
    acc[...] = jnp.zeros_like(acc)
    for copy in copies:
        copy.wait()

    def step(k, carry):
        w = jnp.concatenate([w_s[k, 0], w_s[k, 1], w_s[k, 2], w_s[k, 3], d_s[k].reshape(512, 128)], axis=1)
        acc[...] += jnp.dot(a_s[idx[k]], w, preferred_element_type=f32)
        return carry

    lax.fori_loop(0, 8, step, 0)
    low = acc[:, 512:]
    for q in range(4):
        up = u_s[:, q].reshape(128, 128).astype(f32)
        term = jnp.dot(low, up, precision=lax.Precision.HIGHEST, preferred_element_type=f32)
        cols = slice(128 * q, 128 * q + 128)
        out[:, cols] = (stream[:, cols].astype(f32) + (acc[:, cols] + adapter_scale * term)).astype(bf16)


def m1(idx, hid, own, sib, stream):
    return pl.pallas_call(
        m1_kernel,
        out_shape=jax.ShapeDtypeStruct((512, 512), bf16),
        in_specs=[SMEM] + [ANY] * 24 + [VMEM],
        out_specs=VMEM,
        scratch_shapes=[
            pltpu.VMEM((8, 512, 512), bf16),
            pltpu.VMEM((8, 4, 512, 128), bf16),
            pltpu.VMEM((8, 4, 128, 128), bf16),
            pltpu.VMEM((8, 4, 16, 128), bf16),
            pltpu.VMEM((512, 640), f32),
            pltpu.SemaphoreType.DMA((8,)),
            pltpu.SemaphoreType.DMA((32, 3)),
        ],
        compiler_params=pltpu.CompilerParams(vmem_limit_bytes=40 * 2**20),
        cost_estimate=pl.CostEstimate(flops=2 * 512 * 4096 * 640, bytes_accessed=12 * 2**20, transcendentals=0),
        name="m1",
    )(idx, *hid, *own, *sib, stream)


def m2_kernel(idx, *refs):
    blocks = refs[:8]
    gain, w_in = refs[8:10]
    proj, new_stream = refs[10:12]
    a_s, n_s, w_s, acc, sem_a, sem_w, sem_o = refs[12:]
    a_copies = [pltpu.make_async_copy(blocks[i], a_s.at[i], sem_a.at[i]) for i in range(8)]
    w_copies = [pltpu.make_async_copy(w_in.at[pl.ds(4 * k, 4)], w_s.at[k], sem_w.at[k]) for k in range(8)]
    for copy in a_copies + w_copies:
        copy.start()
    total = jnp.zeros((512, 128), f32)
    for i in range(8):
        a_copies[i].wait()
        block = a_s[i].astype(f32)
        square = block * block
        total += square[:, :128] + square[:, 128:256] + square[:, 256:384] + square[:, 384:]
    rows = pl.multiple_of(64 * idx[9], 64)
    o_copies = [
        pltpu.make_async_copy(a_s.at[idx[k], pl.ds(rows, 64)], new_stream.at[:, pl.ds(512 * k, 512)], sem_o.at[k])
        for k in range(8)
    ]
    for copy in o_copies:
        copy.start()
    scale = lax.rsqrt(jnp.sum(total, axis=1, keepdims=True) * (1.0 / 4096) + norm_eps)
    for k in range(8):
        n_s[k] = (a_s[idx[k]].astype(f32) * scale * gain[:, 512 * k : 512 * k + 512].astype(f32)).astype(bf16)
    acc[...] = jnp.zeros_like(acc)
    for copy in w_copies:
        copy.wait()

    def step(k, carry):
        a = n_s[k]
        for b in range(3):
            acc[b] += jnp.dot(a, w_s[k, :, b].reshape(512, 512), preferred_element_type=f32)
        return carry

    lax.fori_loop(0, 8, step, 0)
    proj[...] = acc[...].astype(bf16)
    for copy in o_copies:
        copy.wait()


def m2(idx, blocks, gain, w_in):
    return pl.pallas_call(
        m2_kernel,
        out_shape=[jax.ShapeDtypeStruct((3, 512, 512), bf16), jax.ShapeDtypeStruct((64, 4096), bf16)],
        in_specs=[SMEM] + [ANY] * 8 + [VMEM, ANY],
        out_specs=[VMEM, ANY],
        scratch_shapes=[
            pltpu.VMEM((8, 512, 512), bf16),
            pltpu.VMEM((8, 512, 512), bf16),
            pltpu.VMEM((8, 4, 3, 128, 512), bf16),
            pltpu.VMEM((3, 512, 512), f32),
            pltpu.SemaphoreType.DMA((8,)),
            pltpu.SemaphoreType.DMA((8,)),
            pltpu.SemaphoreType.DMA((8,)),
        ],
        compiler_params=pltpu.CompilerParams(vmem_limit_bytes=50 * 2**20),
        cost_estimate=pl.CostEstimate(flops=2 * 512 * 4096 * 1536, bytes_accessed=20 * 2**20, transcendentals=0),
        name="m2",
    )(idx, *blocks, gain, w_in)


def dft_tables():
    n = np.arange(256, dtype=np.int64)
    k = np.arange(128, dtype=np.int64)
    angle = (2 * np.pi / 256) * ((k[:, None] * n[None, :]) % 256)
    cos, sin = np.cos(angle), np.sin(angle)
    sin[0] = np.cos(np.pi * n)
    forward = np.concatenate([cos, sin])
    weight = np.full((128, 1), 2.0)
    weight[0] = 1.0
    inverse = (np.concatenate([cos * weight, sin * weight]) / 256.0).T[128:]
    return split_np(forward) + split_np(inverse)


def split_np(table):
    high = table.astype(np.float32).astype(ml_dtypes.bfloat16)
    low = (table - high.astype(np.float64)).astype(np.float32).astype(ml_dtypes.bfloat16)
    return [high, low]


def split(value):
    high = value.astype(bf16)
    return high, (value - high.astype(f32)).astype(bf16)


def dot(a, b):
    return jnp.dot(a, b, preferred_element_type=f32)


def conv_kernel(inner, halo, lead, taps, bias, f_hi, f_lo, g_hi, g_lo, out):
    row = lax.broadcasted_iota(jnp.int32, (128, 512), 0)
    first = row == 0
    h = taps[...] + jnp.where(first, bias[...], 0.0)
    h_hi, h_lo = split(h)
    fh, fl = f_hi[:, :128], f_lo[:, :128]
    spectrum = dot(fh, h_hi) + dot(fh, h_lo) + dot(fl, h_hi)
    h_a, h_b = spectrum[:128], spectrum[128:]
    mixed = jnp.where(first, 0.0, h_b)
    last = jnp.where(first, h_b, h_a)
    for w in range(4):
        if w == 0:
            window = jnp.concatenate([halo[...], inner[:128]], axis=0)
        else:
            window = inner[128 * (w - 1) : 128 * (w + 1)]
        x = dot(f_hi[...], window) + dot(f_lo[...], window)
        x_a, x_b = x[:128], x[128:]
        y_hi, y_lo = split(jnp.concatenate([x_a * h_a - x_b * mixed, x_a * mixed + x_b * last], axis=0))
        y = dot(g_hi[...], y_hi) + dot(g_hi[...], y_lo) + dot(g_lo[...], y_hi)
        rows = slice(128 * w, 128 * w + 128)
        out[rows] = (lead[rows] * y).astype(bf16)


def conv(inner, halo, lead, taps, bias):
    tables = [jnp.asarray(t) for t in dft_tables()]
    return pl.pallas_call(
        conv_kernel,
        out_shape=jax.ShapeDtypeStruct((512, 512), bf16),
        in_specs=[VMEM] * 9,
        out_specs=VMEM,
        compiler_params=pltpu.CompilerParams(vmem_limit_bytes=40 * 2**20),
        cost_estimate=pl.CostEstimate(flops=10**9, bytes_accessed=4 * 2**20, transcendentals=0),
        name="conv",
    )(inner, halo, lead, taps, bias, *tables)


def passed_along(value):
    return lax.ppermute(value, "ctx", [(c, c + 1) for c in range(31)])


def featurize(extended, filters):
    taps = filters.shape[1]
    length = extended.shape[1] - taps + 1
    running = jnp.zeros((extended.shape[0], length, extended.shape[2]), f32)
    for j in range(taps):
        running = running + filters[:, j, None, :] * extended[:, taps - 1 - j : taps - 1 - j + length, :].astype(f32)
    return running


def body(
    previous_hidden,
    output_weight,
    adapter_down_weight,
    adapter_up_weight,
    stream,
    prenorm_gain,
    input_weight,
    short_kernel,
    long_kernel,
    long_direct_bias,
):
    c = lax.axis_index("ctx")
    t = lax.axis_index("tp")
    z, q, core = c // 4, c % 4, c % 2
    y, x = t // 4, t % 4
    s = 1 - 2 * core

    def slot_of(block):
        return 4 * ((block // 4) ^ y) + (s * (x - block % 4)) % 4

    near = (z - s * jnp.arange(8, dtype=jnp.int32)) % 8
    idx1 = jnp.concatenate([slot_of(near), near, core[None]]).astype(jnp.int32)
    idx2 = jnp.concatenate([slot_of(jnp.arange(8, dtype=jnp.int32)), core[None], t[None]]).astype(jnp.int32)

    w_in = lax.all_gather(input_weight, "ctx", axis=0, tiled=False)
    down = lax.dynamic_slice_in_dim(adapter_down_weight, 128 * q, 128, axis=0)
    up = lax.dynamic_slice_in_dim(adapter_up_weight, 128 * c, 128, axis=1)
    weights = sent(jnp.concatenate([output_weight, down, up], axis=0), SWAP)
    hid = gather_tp(previous_hidden)
    other = sent(weights, Y_LO)
    low = (q // 2) == 0
    both = jnp.stack([jnp.where(low, weights, other), jnp.where(low, other, weights)])
    own = gather_z(both)
    sib = [sent(value, CORE) for value in own]
    stream_cols = lax.all_to_all(stream, "tp", split_axis=1, concat_axis=0, tiled=True)
    block = m1(idx1, hid, own, sib, stream_cols)
    blocks = gather_tp(block)
    projected, new_stream = m2(idx2, blocks, prenorm_gain.reshape(1, 4096), w_in)

    earlier = passed_along(projected[:, 506:, :])
    featured = featurize(jnp.concatenate([earlier, projected], axis=1), short_kernel)
    inner = (featured[1] * featured[2]).astype(bf16)
    halo = passed_along(inner[384:])
    mixer_out = conv(inner, halo, featured[0], long_kernel, long_direct_bias.reshape(1, 512))
    return (new_stream, mixer_out)


def solution(mesh):
    in_specs = (
        P("ctx", "tp"),
        P("tp", "ctx"),
        P("tp", None),
        P("tp", None),
        P(("ctx", "tp"), None),
        P(),
        P(None, "ctx", "tp"),
        P(None, None, "tp"),
        P(None, "tp"),
        P("tp"),
    )
    out_specs = (P(("ctx", "tp"), None), P("ctx", "tp"))
    return jax.shard_map(body, mesh=mesh, in_specs=in_specs, out_specs=out_specs, check_vma=False)
```

```python
import functools

import jax
import jax.numpy as jnp
import ml_dtypes
import numpy as np
from jax import lax
from jax.experimental import pallas as pl
from jax.experimental.pallas import tpu as pltpu
from jax.sharding import PartitionSpec as P

adapter_scale = 0.5
norm_eps = 1e-05
f32 = jnp.float32
bf16 = jnp.bfloat16

NZ, NX = 8, 4
ANY = pl.BlockSpec(memory_space=pl.ANY)
VMEM = pl.BlockSpec(memory_space=pltpu.VMEM)
SMEM = pl.BlockSpec(memory_space=pltpu.SMEM)


def joint(move):
    pairs = []
    for c in range(32):
        for t in range(8):
            z, q, y, x = c // 4, c % 4, t // 4, t % 4
            z2, q2, y2, x2 = move(z, q, y, x)
            pairs.append((c * 8 + t, (z2 * 4 + q2) * 8 + y2 * 4 + x2))
    return pairs


def sign(q):
    return 1 - 2 * (q % 2)


X_A = joint(lambda z, q, y, x: (z, q, y, (x + sign(q)) % NX))
X_2 = joint(lambda z, q, y, x: (z, q, y, (x + 2) % NX))
X_B = joint(lambda z, q, y, x: (z, q, y, (x - sign(q)) % NX))
Y_HI = joint(lambda z, q, y, x: (z, q, 1 - y, x))
Z_A = joint(lambda z, q, y, x: ((z + sign(q)) % NZ, q, y, x))
Z_B = joint(lambda z, q, y, x: ((z - sign(q)) % NZ, q, y, x))
CORE = joint(lambda z, q, y, x: (z, q ^ 1, y, x))
Y_LO = joint(lambda z, q, y, x: (z, q ^ 2, y, x))
SWAP = joint(lambda z, q, y, x: (y * 4 + x, q, z // 4, z % 4))


def sent(value, pairs):
    return lax.ppermute(value, ("ctx", "tp"), pairs)


def fence(*values):
    return lax.optimization_barrier(values)


GROUPS = ((0, 1, 7, 2, 6), (3, 5), (4,))
IN_GROUPS = ((0, 1, 7, 2, 6), (3, 5, 4))


def grouped(slots, group):
    return sent(jnp.stack([slots[k] for k in group]), CORE)


def placed(refs, groups):
    where = {k: ref.at[n] for ref, group in zip(refs, groups) for n, k in enumerate(group)}
    return [where[(8 - k) % 8] for k in range(8)]


def m1_kernel(slots, idx, *refs):
    hid, down = refs[:2]
    own = refs[2:10]
    sib = placed(refs[10:13], GROUPS)
    outs = refs[13 : 13 + len(slots)]
    h_s, d_s, w_s, sem, sem_w = refs[13 + len(slots) :]
    copies = [pltpu.make_async_copy(hid, h_s, sem.at[0]), pltpu.make_async_copy(down, d_s, sem.at[1])]
    weights = []
    for k in range(8):
        weights.append([pltpu.make_async_copy(ref, w_s.at[k, i], sem_w.at[k, i]) for i, ref in enumerate((own[k], sib[k]))])
    for copy in copies + sum(weights, []):
        copy.start()
    even = idx[16] == 0
    for copy in copies:
        copy.wait()
    a = jnp.concatenate([h_s[pl.ds(pl.multiple_of(64 * idx[8 + n], 64), 64)] for n in slots], axis=0)
    low = jnp.dot(a, d_s[...], preferred_element_type=f32)
    for i in range(len(slots)):
        outs[i][8, :, :128] = low[64 * i : 64 * i + 64].astype(outs[i].dtype)
        outs[i][8, :, 128:] = jnp.zeros((64, 384), outs[i].dtype)
    for k in range(8):
        for copy in weights[k]:
            copy.wait()
        quarters = []
        for ylo in range(2):
            one, two = w_s[k, 0, ylo], w_s[k, 1, ylo]
            quarters += [jnp.where(even, one, two), jnp.where(even, two, one)]
        sums = jnp.dot(a, jnp.concatenate(quarters, axis=1), preferred_element_type=f32)
        for i in range(len(slots)):
            outs[i][idx[k]] = sums[64 * i : 64 * i + 64].astype(outs[i].dtype)


def m1(slots, idx, hid, down, own, sib):
    block = (9, 64, 512)
    return pl.pallas_call(
        functools.partial(m1_kernel, slots),
        out_shape=[jax.ShapeDtypeStruct(block, bf16 if n else f32) for n in slots],
        in_specs=[SMEM] + [ANY] * 13,
        out_specs=[VMEM] * len(slots),
        scratch_shapes=[
            pltpu.VMEM((512, 512), bf16),
            pltpu.VMEM((512, 128), bf16),
            pltpu.VMEM((8, 2, 2, 512, 128), bf16),
            pltpu.SemaphoreType.DMA((2,)),
            pltpu.SemaphoreType.DMA((8, 2)),
        ],
        compiler_params=pltpu.CompilerParams(vmem_limit_bytes=56 * 2**20),
        cost_estimate=pl.CostEstimate(
            flops=2 * 64 * len(slots) * 512 * 4096, bytes_accessed=(5 + len(slots)) * 2**20, transcendentals=0
        ),
        name="m1",
    )(idx, hid, down, *own, *sib)


def norm_kernel(idx, mine, ra, rb, ry, ups, stream, gain, new_stream, normed, u_s):
    for n, slot in enumerate(UP_SLOTS):
        u_s[idx[8 + slot]] = ups[n]
    whole = mine[...] + (ra[...].astype(f32) + (rb[...].astype(f32) + ry[...].astype(f32)))
    low = whole[8, :, :128] * adapter_scale
    low_hi = low.astype(bf16)
    low_mid = (low - low_hi.astype(f32)).astype(bf16)
    low_lo = (low - low_hi.astype(f32) - low_mid.astype(f32)).astype(bf16)
    lows = jnp.concatenate([low_hi, low_mid, low_lo], axis=1)
    total = jnp.zeros((64, 512), f32)
    parts = []
    for j in range(8):
        up = u_s[:, :, 512 * j : 512 * j + 512].reshape(128, 512)
        term = jnp.dot(lows, jnp.concatenate([up, up, up], axis=0), preferred_element_type=f32)
        summed = stream[j].astype(f32) + (whole[j] + term)
        new_stream[j] = summed.astype(bf16)
        total += summed * summed
        parts.append(summed)
    scale = lax.rsqrt(jnp.sum(total, axis=1, keepdims=True) * (1.0 / 4096) + norm_eps)
    for j in range(8):
        normed[j] = (parts[j] * scale * gain[j].astype(f32)).astype(bf16)


UP_SLOTS = (0, 4, 1, 5, 2, 6, 3, 7)


def norm(idx, mine, ra, rb, ry, ups, stream, gain):
    return pl.pallas_call(
        norm_kernel,
        out_shape=[jax.ShapeDtypeStruct((8, 64, 512), bf16)] * 2,
        in_specs=[SMEM] + [VMEM] * 7,
        out_specs=[VMEM] * 2,
        scratch_shapes=[pltpu.VMEM((8, 16, 4096), bf16)],
        compiler_params=pltpu.CompilerParams(vmem_limit_bytes=24 * 2**20),
        cost_estimate=pl.CostEstimate(flops=2**27, bytes_accessed=2**22, transcendentals=0),
        name="norm",
    )(idx, mine, ra, rb, ry, ups, stream, gain)


def m2_kernel(idx, *refs):
    blocks = refs[:8]
    own = refs[8:16]
    sib = placed(refs[16:18], IN_GROUPS)
    taps = refs[18]
    lead, inner, edge, head, tail = refs[19:24]
    a_s, w_s, acc, p_s, sem_a, sem_w, sem_l = refs[24:]
    core = idx[16]
    copies, weights = [], []
    for n in range(8):
        rows = pl.ds(pl.multiple_of(64 * idx[8 + n], 64), 64)
        copies.append(pltpu.make_async_copy(blocks[n], a_s.at[:, rows], sem_a.at[n]))
        copies[n].start()
    for k in range(8):
        weights.append([])
        for ylo in range(2):
            for i, (ref, c) in enumerate(((own[k], core), (sib[k], 1 - core))):
                weights[k].append(pltpu.make_async_copy(ref.at[ylo], w_s.at[k, ylo, c], sem_w.at[k, ylo, i]))
        for copy in weights[k]:
            copy.start()
    for copy in copies:
        copy.wait()
    def products(step, b):
        span = (2 * step, 2 * step + 1)
        a = jnp.concatenate([a_s[idx[k]] for k in span], axis=1)
        w = w_s[span[0] : span[0] + 2, :, :, b].reshape(1024, 512)
        return jnp.dot(a, w, preferred_element_type=f32)

    for step in range(3):
        for copy in weights[2 * step] + weights[2 * step + 1]:
            copy.wait()
        for b in range(3):
            term = products(step, b)
            acc[b] = acc[b] + term if step else term
    for copy in weights[6] + weights[7]:
        copy.wait()
    for b in range(3):
        p_s[b, :16] = jnp.zeros((16, 512), f32)
        p = (acc[b] + products(3, b)).astype(bf16)
        head[b] = p[:16]
        tail[b] = p[496:]
        p_s[b, 16:] = p.astype(f32)

    def featured(b):
        running = taps[b, 0:1] * p_s[b, 16:528]
        for j in range(1, 7):
            running = running + taps[b, j : j + 1] * p_s[b, 16 - j : 528 - j]
        return running

    acc[0] = featured(0)
    copy = pltpu.make_async_copy(acc.at[0], lead, sem_l)
    copy.start()
    acc[1] = featured(1)
    inner[...] = (acc[1] * featured(2)).astype(bf16)
    edge[...] = inner[384:]
    copy.wait()


def m2(idx, blocks, own, sib, taps):
    return pl.pallas_call(
        m2_kernel,
        out_shape=[
            jax.ShapeDtypeStruct((512, 512), f32),
            jax.ShapeDtypeStruct((512, 512), bf16),
            jax.ShapeDtypeStruct((128, 512), bf16),
            jax.ShapeDtypeStruct((3, 16, 512), bf16),
            jax.ShapeDtypeStruct((3, 16, 512), bf16),
        ],
        in_specs=[SMEM] + [ANY] * 18 + [VMEM],
        out_specs=[ANY] + [VMEM] * 4,
        scratch_shapes=[
            pltpu.VMEM((8, 512, 512), bf16),
            pltpu.VMEM((8, 2, 2, 3, 128, 512), bf16),
            pltpu.VMEM((3, 512, 512), f32),
            pltpu.VMEM((3, 528, 512), f32),
            pltpu.SemaphoreType.DMA((8,)),
            pltpu.SemaphoreType.DMA((8, 2, 2)),
            pltpu.SemaphoreType.DMA,
        ],
        compiler_params=pltpu.CompilerParams(vmem_limit_bytes=56 * 2**20),
        cost_estimate=pl.CostEstimate(flops=2 * 512 * 4096 * 1536, bytes_accessed=20 * 2**20, transcendentals=0),
        name="m2",
    )(idx, *blocks, *own, *sib, taps)


def dft_tables():
    n = np.arange(256, dtype=np.int64)
    k = np.arange(128, dtype=np.int64)
    angle = (2 * np.pi / 256) * ((k[:, None] * n[None, :]) % 256)
    cos, sin = np.cos(angle), np.sin(angle)
    sin[0] = np.cos(np.pi * n)
    forward = np.concatenate([cos, sin])
    weight = np.full((128, 1), 2.0)
    weight[0] = 1.0
    inverse = (np.concatenate([cos * weight, sin * weight]) / 256.0).T[128:]
    return split_np(forward) + split_np(inverse)


def split_np(table):
    high = table.astype(np.float32).astype(ml_dtypes.bfloat16)
    low = (table - high.astype(np.float64)).astype(np.float32).astype(ml_dtypes.bfloat16)
    return [high, low]


def split(value):
    high = value.astype(bf16)
    return high, (value - high.astype(f32)).astype(bf16)


def dot(a, b):
    return jnp.dot(a, b, preferred_element_type=f32)


def conv_kernel(lead, inner, head, earlier, halo, short, taps, bias, f_hi, f_lo, g_hi, g_lo, out, ext):
    first = lax.broadcasted_iota(jnp.int32, (128, 512), 0) == 0
    h = taps[...] + jnp.where(first, bias[...], 0.0)
    h_hi, h_lo = split(h)
    fh, fl = f_hi[:, :128], f_lo[:, :128]
    spectrum = dot(fh, h_hi) + dot(fh, h_lo) + dot(fl, h_hi)
    h_a, h_b = spectrum[:128], spectrum[128:]
    mixed = jnp.where(first, 0.0, h_b)
    last = jnp.where(first, h_b, h_a)
    start = []
    for b in range(3):
        rows = jnp.concatenate([earlier[b], head[b]], axis=0).astype(f32)
        running = short[b, 0:1] * rows[16:]
        for j in range(1, 7):
            running = running + short[b, j : j + 1] * rows[16 - j : 32 - j]
        start.append(running)
    ext[:128] = halo[...]
    ext[128:] = inner[...]
    ext[128:144] = (start[1] * start[2]).astype(bf16)
    for w in range(4):
        window = ext[128 * w : 128 * w + 256]
        x = dot(f_hi[...], window) + dot(f_lo[...], window)
        x_a, x_b = x[:128], x[128:]
        y_hi, y_lo = split(jnp.concatenate([x_a * h_a - x_b * mixed, x_a * mixed + x_b * last], axis=0))
        y = dot(g_hi[...], y_hi) + dot(g_hi[...], y_lo) + dot(g_lo[...], y_hi)
        rows = slice(128 * w, 128 * w + 128)
        out[rows] = (lead[rows] * y).astype(bf16)
        if w == 0:
            out[:16] = (start[0] * y[:16]).astype(bf16)


def conv(lead, inner, head, earlier, halo, short, taps, bias):
    tables = [jnp.asarray(t) for t in dft_tables()]
    return pl.pallas_call(
        conv_kernel,
        out_shape=jax.ShapeDtypeStruct((512, 512), bf16),
        in_specs=[VMEM] * 12,
        out_specs=VMEM,
        scratch_shapes=[pltpu.VMEM((640, 512), bf16)],
        compiler_params=pltpu.CompilerParams(vmem_limit_bytes=56 * 2**20),
        cost_estimate=pl.CostEstimate(flops=10**9, bytes_accessed=4 * 2**20, transcendentals=0),
        name="conv",
    )(lead, inner, head, earlier, halo, short, taps, bias, *tables)


def passed_along(value):
    return lax.ppermute(value, "ctx", [(c, c + 1) for c in range(31)])


def body(
    previous_hidden,
    output_weight,
    adapter_down_weight,
    adapter_up_weight,
    stream,
    prenorm_gain,
    input_weight,
    short_kernel,
    long_kernel,
    long_direct_bias,
):
    c = lax.axis_index("ctx")
    t = lax.axis_index("tp")
    z, q, core = c // 4, c % 4, c % 2
    y, x = t // 4, t % 4
    s = 1 - 2 * core

    near = (z - s * jnp.arange(8, dtype=jnp.int32)) % 8
    slot = np.arange(8, dtype=np.int32)
    places = 4 * (y ^ (slot // 4)) + (x - s * slot) % 4
    idx = jnp.concatenate([near, places, core[None]]).astype(jnp.int32)
    gain = prenorm_gain.reshape(8, 1, 512)
    stream = stream.reshape(64, 8, 512).transpose(1, 0, 2)
    low = (q // 2) == 0

    def pair(value, other):
        return jnp.stack([jnp.where(low, value, other), jnp.where(low, other, value)])

    other = sent(output_weight, Y_LO)
    both = pair(output_weight, other)
    za1, zb1, idx, gain, stream, inputs = fence(
        sent(both, Z_A), sent(both, Z_B), idx, gain, stream, sent(input_weight, Y_LO)
    )
    inputs = pair(input_weight, inputs)
    za2, zb2, inputs = fence(sent(za1, Z_A), sent(zb1, Z_B), inputs)
    sib0 = grouped({0: both, 1: za1, 7: zb1, 2: za2, 6: zb2}, GROUPS[0])
    up = adapter_up_weight[None]
    za3, zb3, sib0, u_y = fence(sent(za2, Z_A), sent(zb2, Z_B), sib0, sent(up, Y_HI))
    up = jnp.concatenate([up, u_y])
    za4, sib1, u_a = fence(sent(za3, Z_A), grouped({3: za3, 5: zb3}, GROUPS[1]), sent(up, X_A))
    up = jnp.concatenate([up, u_a])
    u_2 = sent(up, X_2)
    sib2, inputs = fence(grouped({4: za4}, GROUPS[2]), inputs)
    ia1, ib1 = sent(inputs, Z_A), sent(inputs, Z_B)
    own = [both, za1, za2, za3, za4, zb3, zb2, zb1]
    weights = (idx, previous_hidden, adapter_down_weight, own, [sib0, sib1, sib2])
    p6, p2 = m1((6, 2), *weights)

    def plus(*terms):
        return sum(term.astype(f32) for term in terms).astype(bf16)

    p0, p1, p3, p4, p5, p7 = m1((0, 1, 3, 4, 5, 7), *weights)
    ia2, ib2 = sent(ia1, Z_A), sent(ib1, Z_B)
    r6, r2, p0, p1, p3, p4, p5, p7, u_2 = fence(sent(p6, X_B), sent(p2, X_B), p0, p1, p3, p4, p5, p7, u_2)
    r5, r7, rb = fence(sent(plus(p5, r6), Y_HI), sent(p7, X_A), sent(p3, X_A))
    ra, ry, ia2, ib2 = fence(sent(plus(p1, r2, r5), X_B), sent(plus(p4, r7), Y_HI), ia2, ib2)
    ia3, ib3 = sent(ia2, Z_A), sent(ib2, Z_B)
    up = jnp.concatenate([up, u_2])
    new_stream, block = norm(idx, p0, ra, rb, ry, up, stream, gain)

    a1, b1, y0, ia3, ib3, inputs = fence(
        sent(block, X_A), sent(block, X_B), sent(block, Y_HI), ia3, ib3, inputs
    )
    in0 = grouped({0: inputs, 1: ia1, 7: ib1, 2: ia2, 6: ib2}, IN_GROUPS[0])
    a2, yb1, ya1, ia4 = fence(sent(a1, X_A), sent(y0, X_B), sent(a1, Y_HI), sent(ia3, Z_A))
    ya2, in1, in0 = fence(sent(ya1, X_A), grouped({3: ia3, 5: ib3, 4: ia4}, IN_GROUPS[1]), in0)
    blocks = [block, a1, a2, b1, y0, ya1, ya2, yb1]
    own = [inputs, ia1, ia2, ia3, ia4, ib3, ib2, ib1]
    lead, inner, edge, head, tail = m2(idx, blocks, own, [in0, in1], short_kernel)
    new_stream = new_stream.transpose(1, 0, 2).reshape(64, 4096)
    earlier, halo = passed_along(tail), passed_along(edge)
    mixer_out = conv(lead, inner, head, earlier, halo, short_kernel, long_kernel, long_direct_bias.reshape(1, 512))
    return (new_stream, mixer_out)


def solution(mesh):
    in_specs = (
        P("ctx", "tp"),
        P("tp", "ctx"),
        P("tp", None),
        P("tp", None),
        P(("ctx", "tp"), None),
        P(),
        P(None, "ctx", "tp"),
        P(None, None, "tp"),
        P(None, "tp"),
        P("tp"),
    )
    out_specs = (P(("ctx", "tp"), None), P("ctx", "tp"))
    return jax.shard_map(body, mesh=mesh, in_specs=in_specs, out_specs=out_specs, check_vma=False)
```

```python
import functools

import jax
import jax.numpy as jnp
import ml_dtypes
import numpy as np
from jax import lax
from jax.experimental import pallas as pl
from jax.experimental.pallas import tpu as pltpu
from jax.sharding import PartitionSpec as P

adapter_scale = 0.5
norm_eps = 1e-05
f32 = jnp.float32
bf16 = jnp.bfloat16

NZ, NX = 8, 4
ANY = pl.BlockSpec(memory_space=pl.ANY)
VMEM = pl.BlockSpec(memory_space=pltpu.VMEM)
SMEM = pl.BlockSpec(memory_space=pltpu.SMEM)


def joint(move):
    pairs = []
    for c in range(32):
        for t in range(8):
            z, q, y, x = c // 4, c % 4, t // 4, t % 4
            z2, q2, y2, x2 = move(z, q, y, x)
            pairs.append((c * 8 + t, (z2 * 4 + q2) * 8 + y2 * 4 + x2))
    return pairs


def sign(q):
    return 1 - 2 * (q % 2)


X_A = joint(lambda z, q, y, x: (z, q, y, (x + sign(q)) % NX))
X_2 = joint(lambda z, q, y, x: (z, q, y, (x + 2) % NX))
X_B = joint(lambda z, q, y, x: (z, q, y, (x - sign(q)) % NX))
Y_HI = joint(lambda z, q, y, x: (z, q, 1 - y, x))
Z_A = joint(lambda z, q, y, x: ((z + sign(q)) % NZ, q, y, x))
Z_B = joint(lambda z, q, y, x: ((z - sign(q)) % NZ, q, y, x))
CORE = joint(lambda z, q, y, x: (z, q ^ 1, y, x))
Y_LO = joint(lambda z, q, y, x: (z, q ^ 2, y, x))
SWAP = joint(lambda z, q, y, x: (y * 4 + x, q, z // 4, z % 4))


def sent(value, pairs):
    return lax.ppermute(value, ("ctx", "tp"), pairs)


def fence(*values):
    return lax.optimization_barrier(values)


GROUPS = ((0, 1, 7, 2, 6), (3, 5), (4,))
IN_GROUPS = ((0, 1, 7, 2, 6), (3, 5, 4))


def grouped(slots, group):
    return sent(jnp.stack([slots[k] for k in group]), CORE)


def placed(refs, groups):
    where = {k: ref.at[n] for ref, group in zip(refs, groups) for n, k in enumerate(group)}
    return [where[(8 - k) % 8] for k in range(8)]


def m1_kernel(slots, idx, *refs):
    hid, down = refs[:2]
    own = refs[2:10]
    sib = placed(refs[10:13], GROUPS)
    outs = refs[13 : 13 + len(slots)]
    h_s, d_s, w_s, sem, sem_w = refs[13 + len(slots) :]
    copies = [pltpu.make_async_copy(hid, h_s, sem.at[0]), pltpu.make_async_copy(down, d_s, sem.at[1])]
    weights = []
    for k in range(8):
        weights.append([pltpu.make_async_copy(ref, w_s.at[k, i], sem_w.at[k, i]) for i, ref in enumerate((own[k], sib[k]))])
    for copy in copies + sum(weights, []):
        copy.start()
    even = idx[16] == 0
    for copy in copies:
        copy.wait()
    a = jnp.concatenate([h_s[pl.ds(pl.multiple_of(64 * idx[8 + n], 64), 64)] for n in slots], axis=0)
    low = jnp.dot(a, d_s[...], preferred_element_type=f32)
    for i in range(len(slots)):
        outs[i][8, :, :128] = low[64 * i : 64 * i + 64].astype(outs[i].dtype)
        outs[i][8, :, 128:] = jnp.zeros((64, 384), outs[i].dtype)
    for k in range(8):
        for copy in weights[k]:
            copy.wait()
        quarters = []
        for ylo in range(2):
            one, two = w_s[k, 0, ylo], w_s[k, 1, ylo]
            quarters += [jnp.where(even, one, two), jnp.where(even, two, one)]
        sums = jnp.dot(a, jnp.concatenate(quarters, axis=1), preferred_element_type=f32)
        for i in range(len(slots)):
            outs[i][idx[k]] = sums[64 * i : 64 * i + 64].astype(outs[i].dtype)


def m1(slots, idx, hid, down, own, sib):
    block = (9, 64, 512)
    return pl.pallas_call(
        functools.partial(m1_kernel, slots),
        out_shape=[jax.ShapeDtypeStruct(block, bf16 if n else f32) for n in slots],
        in_specs=[SMEM] + [ANY] * 13,
        out_specs=[VMEM] * len(slots),
        scratch_shapes=[
            pltpu.VMEM((512, 512), bf16),
            pltpu.VMEM((512, 128), bf16),
            pltpu.VMEM((8, 2, 2, 512, 128), bf16),
            pltpu.SemaphoreType.DMA((2,)),
            pltpu.SemaphoreType.DMA((8, 2)),
        ],
        compiler_params=pltpu.CompilerParams(vmem_limit_bytes=56 * 2**20),
        cost_estimate=pl.CostEstimate(
            flops=2 * 64 * len(slots) * 512 * 4096, bytes_accessed=(5 + len(slots)) * 2**20, transcendentals=0
        ),
        name="m1",
    )(idx, hid, down, *own, *sib)


def norm_kernel(idx, mine, ra, rb, ry, ups, stream, gain, new_stream, normed, u_s):
    for n, slot in enumerate(UP_SLOTS):
        u_s[idx[8 + slot]] = ups[n]
    whole = mine[...] + (ra[...].astype(f32) + (rb[...].astype(f32) + ry[...].astype(f32)))
    low = whole[8, :, :128] * adapter_scale
    low_hi = low.astype(bf16)
    low_mid = (low - low_hi.astype(f32)).astype(bf16)
    low_lo = (low - low_hi.astype(f32) - low_mid.astype(f32)).astype(bf16)
    lows = jnp.concatenate([low_hi, low_mid, low_lo], axis=1)
    total = jnp.zeros((64, 512), f32)
    parts = []
    for j in range(8):
        up = u_s[:, :, 512 * j : 512 * j + 512].reshape(128, 512)
        term = jnp.dot(lows, jnp.concatenate([up, up, up], axis=0), preferred_element_type=f32)
        summed = stream[j].astype(f32) + (whole[j] + term)
        new_stream[j] = summed.astype(bf16)
        total += summed * summed
        parts.append(summed)
    scale = lax.rsqrt(jnp.sum(total, axis=1, keepdims=True) * (1.0 / 4096) + norm_eps)
    for j in range(8):
        normed[j] = (parts[j] * scale * gain[j].astype(f32)).astype(bf16)


UP_SLOTS = (0, 4, 1, 5, 2, 6, 3, 7)


def norm(idx, mine, ra, rb, ry, ups, stream, gain):
    return pl.pallas_call(
        norm_kernel,
        out_shape=[jax.ShapeDtypeStruct((8, 64, 512), bf16)] * 2,
        in_specs=[SMEM] + [VMEM] * 7,
        out_specs=[VMEM] * 2,
        scratch_shapes=[pltpu.VMEM((8, 16, 4096), bf16)],
        compiler_params=pltpu.CompilerParams(vmem_limit_bytes=24 * 2**20),
        cost_estimate=pl.CostEstimate(flops=2**27, bytes_accessed=2**22, transcendentals=0),
        name="norm",
    )(idx, mine, ra, rb, ry, ups, stream, gain)


def m2_kernel(idx, *refs):
    blocks = refs[:8]
    own = refs[8:16]
    sib = placed(refs[16:18], IN_GROUPS)
    taps = refs[18]
    lead, inner, edge, head, tail = refs[19:24]
    a_s, w_s, acc, p_s, sem_a, sem_w, sem_l = refs[24:]
    core = idx[16]
    copies, weights = [], []
    for n in range(8):
        rows = pl.ds(pl.multiple_of(64 * idx[8 + n], 64), 64)
        copies.append(pltpu.make_async_copy(blocks[n], a_s.at[:, rows], sem_a.at[n]))
        copies[n].start()
    for k in range(8):
        weights.append([])
        for ylo in range(2):
            for i, (ref, c) in enumerate(((own[k], core), (sib[k], 1 - core))):
                weights[k].append(pltpu.make_async_copy(ref.at[ylo], w_s.at[k, ylo, c], sem_w.at[k, ylo, i]))
        for copy in weights[k]:
            copy.start()
    for copy in copies:
        copy.wait()
    def products(step, b):
        span = (2 * step, 2 * step + 1)
        a = jnp.concatenate([a_s[idx[k]] for k in span], axis=1)
        w = w_s[span[0] : span[0] + 2, :, :, b].reshape(1024, 512)
        return jnp.dot(a, w, preferred_element_type=f32)

    for step in range(3):
        for copy in weights[2 * step] + weights[2 * step + 1]:
            copy.wait()
        for b in range(3):
            term = products(step, b)
            acc[b] = acc[b] + term if step else term
    for copy in weights[6] + weights[7]:
        copy.wait()
    for b in range(3):
        p_s[b, :16] = jnp.zeros((16, 512), f32)
        p = (acc[b] + products(3, b)).astype(bf16)
        head[b] = p[:16]
        tail[b] = p[496:]
        p_s[b, 16:] = p.astype(f32)

    def featured(b):
        running = taps[b, 0:1] * p_s[b, 16:528]
        for j in range(1, 7):
            running = running + taps[b, j : j + 1] * p_s[b, 16 - j : 528 - j]
        return running

    acc[0] = featured(0)
    copy = pltpu.make_async_copy(acc.at[0], lead, sem_l)
    copy.start()
    acc[1] = featured(1)
    inner[...] = (acc[1] * featured(2)).astype(bf16)
    edge[...] = inner[384:]
    copy.wait()


def m2(idx, blocks, own, sib, taps):
    return pl.pallas_call(
        m2_kernel,
        out_shape=[
            jax.ShapeDtypeStruct((512, 512), f32),
            jax.ShapeDtypeStruct((512, 512), bf16),
            jax.ShapeDtypeStruct((128, 512), bf16),
            jax.ShapeDtypeStruct((3, 16, 512), bf16),
            jax.ShapeDtypeStruct((3, 16, 512), bf16),
        ],
        in_specs=[SMEM] + [ANY] * 18 + [VMEM],
        out_specs=[ANY] + [VMEM] * 4,
        scratch_shapes=[
            pltpu.VMEM((8, 512, 512), bf16),
            pltpu.VMEM((8, 2, 2, 3, 128, 512), bf16),
            pltpu.VMEM((3, 512, 512), f32),
            pltpu.VMEM((3, 528, 512), f32),
            pltpu.SemaphoreType.DMA((8,)),
            pltpu.SemaphoreType.DMA((8, 2, 2)),
            pltpu.SemaphoreType.DMA,
        ],
        compiler_params=pltpu.CompilerParams(vmem_limit_bytes=36 * 2**20),
        cost_estimate=pl.CostEstimate(flops=2 * 512 * 4096 * 1536, bytes_accessed=20 * 2**20, transcendentals=0),
        name="m2",
    )(idx, *blocks, *own, *sib, taps)


def dft_tables():
    n = np.arange(256, dtype=np.int64)
    k = np.arange(128, dtype=np.int64)
    angle = (2 * np.pi / 256) * ((k[:, None] * n[None, :]) % 256)
    cos, sin = np.cos(angle), np.sin(angle)
    sin[0] = np.cos(np.pi * n)
    forward = np.concatenate([cos, sin])
    weight = np.full((128, 1), 2.0)
    weight[0] = 1.0
    inverse = (np.concatenate([cos * weight, sin * weight]) / 256.0).T[128:]
    return split_np(forward) + split_np(inverse)


def split_np(table):
    high = table.astype(np.float32).astype(ml_dtypes.bfloat16)
    low = (table - high.astype(np.float64)).astype(np.float32).astype(ml_dtypes.bfloat16)
    return [high, low]


def split(value):
    high = value.astype(bf16)
    return high, (value - high.astype(f32)).astype(bf16)


def dot(a, b):
    return jnp.dot(a, b, preferred_element_type=f32)


def conv_kernel(lead, inner, head, earlier, halo, short, taps, bias, f_hi, f_lo, g_hi, g_lo, out, ext):
    first = lax.broadcasted_iota(jnp.int32, (128, 512), 0) == 0
    h = taps[...] + jnp.where(first, bias[...], 0.0)
    h_hi, h_lo = split(h)
    fh, fl = f_hi[:, :128], f_lo[:, :128]
    spectrum = dot(fh, h_hi) + dot(fh, h_lo) + dot(fl, h_hi)
    h_a, h_b = spectrum[:128], spectrum[128:]
    mixed = jnp.where(first, 0.0, h_b)
    last = jnp.where(first, h_b, h_a)
    start = []
    for b in range(3):
        rows = jnp.concatenate([earlier[b], head[b]], axis=0).astype(f32)
        running = short[b, 0:1] * rows[16:]
        for j in range(1, 7):
            running = running + short[b, j : j + 1] * rows[16 - j : 32 - j]
        start.append(running)
    ext[:128] = halo[...]
    ext[128:] = inner[...]
    ext[128:144] = (start[1] * start[2]).astype(bf16)
    for w in range(4):
        window = ext[128 * w : 128 * w + 256]
        x = dot(f_hi[...], window) + dot(f_lo[...], window)
        x_a, x_b = x[:128], x[128:]
        y_hi, y_lo = split(jnp.concatenate([x_a * h_a - x_b * mixed, x_a * mixed + x_b * last], axis=0))
        y = dot(g_hi[...], y_hi) + dot(g_hi[...], y_lo) + dot(g_lo[...], y_hi)
        rows = slice(128 * w, 128 * w + 128)
        out[rows] = (lead[rows] * y).astype(bf16)
        if w == 0:
            out[:16] = (start[0] * y[:16]).astype(bf16)


def conv(lead, inner, head, earlier, halo, short, taps, bias):
    tables = [jnp.asarray(t) for t in dft_tables()]
    return pl.pallas_call(
        conv_kernel,
        out_shape=jax.ShapeDtypeStruct((512, 512), bf16),
        in_specs=[VMEM] * 12,
        out_specs=VMEM,
        scratch_shapes=[pltpu.VMEM((640, 512), bf16)],
        compiler_params=pltpu.CompilerParams(vmem_limit_bytes=56 * 2**20),
        cost_estimate=pl.CostEstimate(flops=10**9, bytes_accessed=4 * 2**20, transcendentals=0),
        name="conv",
    )(lead, inner, head, earlier, halo, short, taps, bias, *tables)


def passed_along(value):
    return lax.ppermute(value, "ctx", [(c, c + 1) for c in range(31)])


def body(
    previous_hidden,
    output_weight,
    adapter_down_weight,
    adapter_up_weight,
    stream,
    prenorm_gain,
    input_weight,
    short_kernel,
    long_kernel,
    long_direct_bias,
):
    c = lax.axis_index("ctx")
    t = lax.axis_index("tp")
    z, q, core = c // 4, c % 4, c % 2
    y, x = t // 4, t % 4
    s = 1 - 2 * core

    near = (z - s * jnp.arange(8, dtype=jnp.int32)) % 8
    slot = np.arange(8, dtype=np.int32)
    places = 4 * (y ^ (slot // 4)) + (x - s * slot) % 4
    idx = jnp.concatenate([near, places, core[None]]).astype(jnp.int32)
    gain = prenorm_gain.reshape(8, 1, 512)
    stream = stream.reshape(64, 8, 512).transpose(1, 0, 2)
    low = (q // 2) == 0

    def pair(value, other):
        return jnp.stack([jnp.where(low, value, other), jnp.where(low, other, value)])

    other = sent(output_weight, Y_LO)
    both = pair(output_weight, other)
    up = adapter_up_weight[None]
    za1, zb1, idx, gain, stream, inputs, u_y = fence(
        sent(both, Z_A), sent(both, Z_B), idx, gain, stream, sent(input_weight, Y_LO), sent(up, Y_HI)
    )
    inputs = pair(input_weight, inputs)
    up = jnp.concatenate([up, u_y])
    za2, zb2, inputs, u_a = fence(sent(za1, Z_A), sent(zb1, Z_B), inputs, sent(up, X_A))
    up = jnp.concatenate([up, u_a])
    sib0 = grouped({0: both, 1: za1, 7: zb1, 2: za2, 6: zb2}, GROUPS[0])
    u_2 = sent(up, X_2)
    za3, zb3, sib0 = fence(sent(za2, Z_A), sent(zb2, Z_B), sib0)
    za4, sib1, u_2 = fence(sent(za3, Z_A), grouped({3: za3, 5: zb3}, GROUPS[1]), u_2)
    sib2, inputs = fence(grouped({4: za4}, GROUPS[2]), inputs)
    ia1, ib1 = sent(inputs, Z_A), sent(inputs, Z_B)
    own = [both, za1, za2, za3, za4, zb3, zb2, zb1]
    weights = (idx, previous_hidden, adapter_down_weight, own, [sib0, sib1, sib2])
    p6, p2 = m1((6, 2), *weights)

    def plus(*terms):
        return sum(term.astype(f32) for term in terms).astype(bf16)

    p0, p1, p3, p4, p5, p7 = m1((0, 1, 3, 4, 5, 7), *weights)
    ia2, ib2 = sent(ia1, Z_A), sent(ib1, Z_B)
    r6, r2, p0, p1, p3, p4, p5, p7 = fence(sent(p6, X_B), sent(p2, X_B), p0, p1, p3, p4, p5, p7)
    r5, r7, rb = fence(sent(plus(p5, r6), Y_HI), sent(p7, X_A), sent(p3, X_A))
    ra, ry = fence(sent(plus(p1, r2, r5), X_B), sent(plus(p4, r7), Y_HI))
    ia3, ib3 = sent(ia2, Z_A), sent(ib2, Z_B)
    up = jnp.concatenate([up, u_2])
    new_stream, block = norm(idx, p0, ra, rb, ry, up, stream, gain)

    a1, b1, y0, ia3, ib3, inputs = fence(
        sent(block, X_A), sent(block, X_B), sent(block, Y_HI), ia3, ib3, inputs
    )
    in0 = grouped({0: inputs, 1: ia1, 7: ib1, 2: ia2, 6: ib2}, IN_GROUPS[0])
    a2, yb1, ya1, ia4 = fence(sent(a1, X_A), sent(y0, X_B), sent(a1, Y_HI), sent(ia3, Z_A))
    ya2, in1, in0 = fence(sent(ya1, X_A), grouped({3: ia3, 5: ib3, 4: ia4}, IN_GROUPS[1]), in0)
    blocks = [block, a1, a2, b1, y0, ya1, ya2, yb1]
    own = [inputs, ia1, ia2, ia3, ia4, ib3, ib2, ib1]
    lead, inner, edge, head, tail = m2(idx, blocks, own, [in0, in1], short_kernel)
    new_stream = new_stream.transpose(1, 0, 2).reshape(64, 4096)
    earlier, halo = passed_along(tail), passed_along(edge)
    mixer_out = conv(lead, inner, head, earlier, halo, short_kernel, long_kernel, long_direct_bias.reshape(1, 512))
    return (new_stream, mixer_out)


def solution(mesh):
    in_specs = (
        P("ctx", "tp"),
        P("tp", "ctx"),
        P("tp", None),
        P("tp", None),
        P(("ctx", "tp"), None),
        P(),
        P(None, "ctx", "tp"),
        P(None, None, "tp"),
        P(None, "tp"),
        P("tp"),
    )
    out_specs = (P(("ctx", "tp"), None), P("ctx", "tp"))
    return jax.shard_map(body, mesh=mesh, in_specs=in_specs, out_specs=out_specs, check_vma=False)
```

```python
import functools

import jax
import jax.numpy as jnp
import ml_dtypes
import numpy as np
from jax import lax
from jax.experimental import pallas as pl
from jax.experimental.pallas import tpu as pltpu
from jax.sharding import PartitionSpec as P

adapter_scale = 0.5
norm_eps = 1e-05
f32 = jnp.float32
bf16 = jnp.bfloat16

NZ, NX = 8, 4
ANY = pl.BlockSpec(memory_space=pl.ANY)
VMEM = pl.BlockSpec(memory_space=pltpu.VMEM)
SMEM = pl.BlockSpec(memory_space=pltpu.SMEM)


def joint(move):
    pairs = []
    for c in range(32):
        for t in range(8):
            z, q, y, x = c // 4, c % 4, t // 4, t % 4
            z2, q2, y2, x2 = move(z, q, y, x)
            pairs.append((c * 8 + t, (z2 * 4 + q2) * 8 + y2 * 4 + x2))
    return pairs


def sign(q):
    return 1 - 2 * (q % 2)


X_A = joint(lambda z, q, y, x: (z, q, y, (x + sign(q)) % NX))
X_2 = joint(lambda z, q, y, x: (z, q, y, (x + 2) % NX))
X_B = joint(lambda z, q, y, x: (z, q, y, (x - sign(q)) % NX))
Y_HI = joint(lambda z, q, y, x: (z, q, 1 - y, x))
Z_A = joint(lambda z, q, y, x: ((z + sign(q)) % NZ, q, y, x))
Z_B = joint(lambda z, q, y, x: ((z - sign(q)) % NZ, q, y, x))
CORE = joint(lambda z, q, y, x: (z, q ^ 1, y, x))
Y_LO = joint(lambda z, q, y, x: (z, q ^ 2, y, x))
SWAP = joint(lambda z, q, y, x: (y * 4 + x, q, z // 4, z % 4))


def sent(value, pairs):
    return lax.ppermute(value, ("ctx", "tp"), pairs)


def fence(*values):
    return lax.optimization_barrier(values)


GROUPS = ((0, 1, 7, 2, 6), (3, 5), (4,))
IN_GROUPS = ((0, 1, 7, 2, 6), (3, 5, 4))


def grouped(slots, group):
    return sent(jnp.stack([slots[k] for k in group]), CORE)


def placed(refs, groups):
    where = {k: ref.at[n] for ref, group in zip(refs, groups) for n, k in enumerate(group)}
    return [where[(8 - k) % 8] for k in range(8)]


def m1_kernel(slots, idx, *refs):
    hid, down = refs[:2]
    own = refs[2:10]
    sib = placed(refs[10:13], GROUPS)
    outs = refs[13 : 13 + len(slots)]
    h_s, d_s, w_s, sem, sem_w = refs[13 + len(slots) :]
    copies = [pltpu.make_async_copy(hid, h_s, sem.at[0]), pltpu.make_async_copy(down, d_s, sem.at[1])]
    weights = []
    for k in range(8):
        weights.append([pltpu.make_async_copy(ref, w_s.at[k, i], sem_w.at[k, i]) for i, ref in enumerate((own[k], sib[k]))])
    for copy in copies + sum(weights, []):
        copy.start()
    even = idx[16] == 0
    for copy in copies:
        copy.wait()
    a = jnp.concatenate([h_s[pl.ds(pl.multiple_of(64 * idx[8 + n], 64), 64)] for n in slots], axis=0)
    low = jnp.dot(a, d_s[...], preferred_element_type=f32)
    for i in range(len(slots)):
        outs[i][8, :, :128] = low[64 * i : 64 * i + 64].astype(outs[i].dtype)
        outs[i][8, :, 128:] = jnp.zeros((64, 384), outs[i].dtype)
    for k in range(8):
        for copy in weights[k]:
            copy.wait()
        quarters = []
        for ylo in range(2):
            one, two = w_s[k, 0, ylo], w_s[k, 1, ylo]
            quarters += [jnp.where(even, one, two), jnp.where(even, two, one)]
        sums = jnp.dot(a, jnp.concatenate(quarters, axis=1), preferred_element_type=f32)
        for i in range(len(slots)):
            outs[i][idx[k]] = sums[64 * i : 64 * i + 64].astype(outs[i].dtype)


def m1(slots, idx, hid, down, own, sib):
    block = (9, 64, 512)
    return pl.pallas_call(
        functools.partial(m1_kernel, slots),
        out_shape=[jax.ShapeDtypeStruct(block, bf16 if n else f32) for n in slots],
        in_specs=[SMEM] + [ANY] * 13,
        out_specs=[VMEM] * len(slots),
        scratch_shapes=[
            pltpu.VMEM((512, 512), bf16),
            pltpu.VMEM((512, 128), bf16),
            pltpu.VMEM((8, 2, 2, 512, 128), bf16),
            pltpu.SemaphoreType.DMA((2,)),
            pltpu.SemaphoreType.DMA((8, 2)),
        ],
        compiler_params=pltpu.CompilerParams(vmem_limit_bytes=32 * 2**20),
        cost_estimate=pl.CostEstimate(
            flops=2 * 64 * len(slots) * 512 * 4096, bytes_accessed=(5 + len(slots)) * 2**20, transcendentals=0
        ),
        name="m1",
    )(idx, hid, down, *own, *sib)


def norm_kernel(idx, mine, ra, rb, ry, ups, stream, gain, new_stream, normed, u_s):
    for n, slot in enumerate(UP_SLOTS):
        u_s[idx[8 + slot]] = ups[n]
    whole = mine[...] + (ra[...].astype(f32) + (rb[...].astype(f32) + ry[...].astype(f32)))
    low = whole[8, :, :128] * adapter_scale
    low_hi = low.astype(bf16)
    low_mid = (low - low_hi.astype(f32)).astype(bf16)
    low_lo = (low - low_hi.astype(f32) - low_mid.astype(f32)).astype(bf16)
    lows = jnp.concatenate([low_hi, low_mid, low_lo], axis=1)
    total = jnp.zeros((64, 512), f32)
    parts = []
    for j in range(8):
        up = u_s[:, :, 512 * j : 512 * j + 512].reshape(128, 512)
        term = jnp.dot(lows, jnp.concatenate([up, up, up], axis=0), preferred_element_type=f32)
        summed = stream[j].astype(f32) + (whole[j] + term)
        new_stream[j] = summed.astype(bf16)
        total += summed * summed
        parts.append(summed)
    scale = lax.rsqrt(jnp.sum(total, axis=1, keepdims=True) * (1.0 / 4096) + norm_eps)
    for j in range(8):
        normed[j] = (parts[j] * scale * gain[j].astype(f32)).astype(bf16)


UP_SLOTS = (0, 4, 1, 5, 2, 6, 3, 7)


def norm(idx, mine, ra, rb, ry, ups, stream, gain):
    return pl.pallas_call(
        norm_kernel,
        out_shape=[jax.ShapeDtypeStruct((8, 64, 512), bf16)] * 2,
        in_specs=[SMEM] + [VMEM] * 7,
        out_specs=[VMEM] * 2,
        scratch_shapes=[pltpu.VMEM((8, 16, 4096), bf16)],
        compiler_params=pltpu.CompilerParams(vmem_limit_bytes=24 * 2**20),
        cost_estimate=pl.CostEstimate(flops=2**27, bytes_accessed=2**22, transcendentals=0),
        name="norm",
    )(idx, mine, ra, rb, ry, ups, stream, gain)


def m2_kernel(idx, *refs):
    blocks = refs[:8]
    own = refs[8:16]
    sib = placed(refs[16:18], IN_GROUPS)
    taps = refs[18]
    lead, inner, edge, head, tail = refs[19:24]
    a_s, w_s, acc, p_s, sem_a, sem_w, sem_l = refs[24:]
    core = idx[16]
    copies, weights = [], []
    for n in range(8):
        rows = pl.ds(pl.multiple_of(64 * idx[8 + n], 64), 64)
        copies.append(pltpu.make_async_copy(blocks[n], a_s.at[:, rows], sem_a.at[n]))
        copies[n].start()
    for k in range(8):
        weights.append([])
        for ylo in range(2):
            for i, (ref, c) in enumerate(((own[k], core), (sib[k], 1 - core))):
                weights[k].append(pltpu.make_async_copy(ref.at[ylo], w_s.at[k, ylo, c], sem_w.at[k, ylo, i]))
        for copy in weights[k]:
            copy.start()
    for copy in copies:
        copy.wait()
    def products(step, b):
        span = (2 * step, 2 * step + 1)
        a = jnp.concatenate([a_s[idx[k]] for k in span], axis=1)
        w = w_s[span[0] : span[0] + 2, :, :, b].reshape(1024, 512)
        return jnp.dot(a, w, preferred_element_type=f32)

    for step in range(3):
        for copy in weights[2 * step] + weights[2 * step + 1]:
            copy.wait()
        for b in range(3):
            term = products(step, b)
            acc[b] = acc[b] + term if step else term
    for copy in weights[6] + weights[7]:
        copy.wait()
    for b in range(3):
        p_s[b, :16] = jnp.zeros((16, 512), f32)
        p = (acc[b] + products(3, b)).astype(bf16)
        head[b] = p[:16]
        tail[b] = p[496:]
        p_s[b, 16:] = p.astype(f32)

    def featured(b):
        running = taps[b, 0:1] * p_s[b, 16:528]
        for j in range(1, 7):
            running = running + taps[b, j : j + 1] * p_s[b, 16 - j : 528 - j]
        return running

    acc[0] = featured(0)
    copy = pltpu.make_async_copy(acc.at[0], lead, sem_l)
    copy.start()
    acc[1] = featured(1)
    inner[...] = (acc[1] * featured(2)).astype(bf16)
    edge[...] = inner[384:]
    copy.wait()


def m2(idx, blocks, own, sib, taps):
    return pl.pallas_call(
        m2_kernel,
        out_shape=[
            jax.ShapeDtypeStruct((512, 512), f32),
            jax.ShapeDtypeStruct((512, 512), bf16),
            jax.ShapeDtypeStruct((128, 512), bf16),
            jax.ShapeDtypeStruct((3, 16, 512), bf16),
            jax.ShapeDtypeStruct((3, 16, 512), bf16),
        ],
        in_specs=[SMEM] + [ANY] * 18 + [VMEM],
        out_specs=[ANY] + [VMEM] * 4,
        scratch_shapes=[
            pltpu.VMEM((8, 512, 512), bf16),
            pltpu.VMEM((8, 2, 2, 3, 128, 512), bf16),
            pltpu.VMEM((3, 512, 512), f32),
            pltpu.VMEM((3, 528, 512), f32),
            pltpu.SemaphoreType.DMA((8,)),
            pltpu.SemaphoreType.DMA((8, 2, 2)),
            pltpu.SemaphoreType.DMA,
        ],
        compiler_params=pltpu.CompilerParams(vmem_limit_bytes=36 * 2**20),
        cost_estimate=pl.CostEstimate(flops=2 * 512 * 4096 * 1536, bytes_accessed=20 * 2**20, transcendentals=0),
        name="m2",
    )(idx, *blocks, *own, *sib, taps)


def dft_tables():
    n = np.arange(256, dtype=np.int64)
    k = np.arange(128, dtype=np.int64)
    angle = (2 * np.pi / 256) * ((k[:, None] * n[None, :]) % 256)
    cos, sin = np.cos(angle), np.sin(angle)
    sin[0] = np.cos(np.pi * n)
    forward = np.concatenate([cos, sin])
    weight = np.full((128, 1), 2.0)
    weight[0] = 1.0
    inverse = (np.concatenate([cos * weight, sin * weight]) / 256.0).T[128:]
    return split_np(forward) + split_np(inverse)


def split_np(table):
    high = table.astype(np.float32).astype(ml_dtypes.bfloat16)
    low = (table - high.astype(np.float64)).astype(np.float32).astype(ml_dtypes.bfloat16)
    return [high, low]


def split(value):
    high = value.astype(bf16)
    return high, (value - high.astype(f32)).astype(bf16)


def dot(a, b):
    return jnp.dot(a, b, preferred_element_type=f32)


def conv_kernel(lead, inner, head, earlier, halo, short, taps, bias, f_hi, f_lo, g_hi, g_lo, out, ext):
    first = lax.broadcasted_iota(jnp.int32, (128, 512), 0) == 0
    h = taps[...] + jnp.where(first, bias[...], 0.0)
    h_hi, h_lo = split(h)
    fh, fl = f_hi[:, :128], f_lo[:, :128]
    spectrum = dot(fh, h_hi) + dot(fh, h_lo) + dot(fl, h_hi)
    h_a, h_b = spectrum[:128], spectrum[128:]
    mixed = jnp.where(first, 0.0, h_b)
    last = jnp.where(first, h_b, h_a)
    start = []
    for b in range(3):
        rows = jnp.concatenate([earlier[b], head[b]], axis=0).astype(f32)
        running = short[b, 0:1] * rows[16:]
        for j in range(1, 7):
            running = running + short[b, j : j + 1] * rows[16 - j : 32 - j]
        start.append(running)
    ext[:128] = halo[...]
    ext[128:] = inner[...]
    ext[128:144] = (start[1] * start[2]).astype(bf16)
    for w in range(4):
        window = ext[128 * w : 128 * w + 256]
        x = dot(f_hi[...], window) + dot(f_lo[...], window)
        x_a, x_b = x[:128], x[128:]
        y_hi, y_lo = split(jnp.concatenate([x_a * h_a - x_b * mixed, x_a * mixed + x_b * last], axis=0))
        y = dot(g_hi[...], y_hi) + dot(g_hi[...], y_lo) + dot(g_lo[...], y_hi)
        rows = slice(128 * w, 128 * w + 128)
        out[rows] = (lead[rows] * y).astype(bf16)
        if w == 0:
            out[:16] = (start[0] * y[:16]).astype(bf16)


def conv(lead, inner, head, earlier, halo, short, taps, bias):
    tables = [jnp.asarray(t) for t in dft_tables()]
    return pl.pallas_call(
        conv_kernel,
        out_shape=jax.ShapeDtypeStruct((512, 512), bf16),
        in_specs=[VMEM] * 12,
        out_specs=VMEM,
        scratch_shapes=[pltpu.VMEM((640, 512), bf16)],
        compiler_params=pltpu.CompilerParams(vmem_limit_bytes=56 * 2**20),
        cost_estimate=pl.CostEstimate(flops=10**9, bytes_accessed=4 * 2**20, transcendentals=0),
        name="conv",
    )(lead, inner, head, earlier, halo, short, taps, bias, *tables)


def passed_along(value):
    return lax.ppermute(value, "ctx", [(c, c + 1) for c in range(31)])


def body(
    previous_hidden,
    output_weight,
    adapter_down_weight,
    adapter_up_weight,
    stream,
    prenorm_gain,
    input_weight,
    short_kernel,
    long_kernel,
    long_direct_bias,
):
    c = lax.axis_index("ctx")
    t = lax.axis_index("tp")
    z, q, core = c // 4, c % 4, c % 2
    y, x = t // 4, t % 4
    s = 1 - 2 * core

    near = (z - s * jnp.arange(8, dtype=jnp.int32)) % 8
    slot = np.arange(8, dtype=np.int32)
    places = 4 * (y ^ (slot // 4)) + (x - s * slot) % 4
    idx = jnp.concatenate([near, places, core[None]]).astype(jnp.int32)
    gain = prenorm_gain.reshape(8, 1, 512)
    stream = stream.reshape(64, 8, 512).transpose(1, 0, 2)
    low = (q // 2) == 0

    def pair(value, other):
        return jnp.stack([jnp.where(low, value, other), jnp.where(low, other, value)])

    other = sent(output_weight, Y_LO)
    both = pair(output_weight, other)
    up = adapter_up_weight[None]
    za1, zb1, idx, gain, stream, inputs, u_y = fence(
        sent(both, Z_A), sent(both, Z_B), idx, gain, stream, sent(input_weight, Y_LO), sent(up, Y_HI)
    )
    inputs = pair(input_weight, inputs)
    up = jnp.concatenate([up, u_y])
    za2, zb2, inputs, u_a = fence(sent(za1, Z_A), sent(zb1, Z_B), inputs, sent(up, X_A))
    up = jnp.concatenate([up, u_a])
    sib0 = grouped({0: both, 1: za1, 7: zb1, 2: za2, 6: zb2}, GROUPS[0])
    u_2 = sent(up, X_2)
    za3, zb3, sib0 = fence(sent(za2, Z_A), sent(zb2, Z_B), sib0)
    za4, sib1, u_2 = fence(sent(za3, Z_A), grouped({3: za3, 5: zb3}, GROUPS[1]), u_2)
    sib2, inputs = fence(grouped({4: za4}, GROUPS[2]), inputs)
    ia1, ib1 = sent(inputs, Z_A), sent(inputs, Z_B)
    own = [both, za1, za2, za3, za4, zb3, zb2, zb1]
    weights = (idx, previous_hidden, adapter_down_weight, own, [sib0, sib1, sib2])
    p6, p2 = m1((6, 2), *weights)

    def plus(*terms):
        return sum(term.astype(f32) for term in terms).astype(bf16)

    p0, p1, p3, p4, p5, p7 = m1((0, 1, 3, 4, 5, 7), *weights)
    ia2, ib2 = sent(ia1, Z_A), sent(ib1, Z_B)
    r6, r2, p0, p1, p3, p4, p5, p7 = fence(sent(p6, X_B), sent(p2, X_B), p0, p1, p3, p4, p5, p7)
    r5, r7, rb = fence(sent(plus(p5, r6), Y_HI), sent(p7, X_A), sent(p3, X_A))
    ra, ry = fence(sent(plus(p1, r2, r5), X_B), sent(plus(p4, r7), Y_HI))
    ia3, ib3 = sent(ia2, Z_A), sent(ib2, Z_B)
    up = jnp.concatenate([up, u_2])
    new_stream, block = norm(idx, p0, ra, rb, ry, up, stream, gain)

    a1, b1, y0, ia3, ib3, inputs = fence(
        sent(block, X_A), sent(block, X_B), sent(block, Y_HI), ia3, ib3, inputs
    )
    in0 = grouped({0: inputs, 1: ia1, 7: ib1, 2: ia2, 6: ib2}, IN_GROUPS[0])
    a2, yb1, ya1, ia4 = fence(sent(a1, X_A), sent(y0, X_B), sent(a1, Y_HI), sent(ia3, Z_A))
    ya2, in1, in0 = fence(sent(ya1, X_A), grouped({3: ia3, 5: ib3, 4: ia4}, IN_GROUPS[1]), in0)
    blocks = [block, a1, a2, b1, y0, ya1, ya2, yb1]
    own = [inputs, ia1, ia2, ia3, ia4, ib3, ib2, ib1]
    lead, inner, edge, head, tail = m2(idx, blocks, own, [in0, in1], short_kernel)
    new_stream = new_stream.transpose(1, 0, 2).reshape(64, 4096)
    earlier, halo = passed_along(tail), passed_along(edge)
    mixer_out = conv(lead, inner, head, earlier, halo, short_kernel, long_kernel, long_direct_bias.reshape(1, 512))
    return (new_stream, mixer_out)


def solution(mesh):
    in_specs = (
        P("ctx", "tp"),
        P("tp", "ctx"),
        P("tp", None),
        P("tp", None),
        P(("ctx", "tp"), None),
        P(),
        P(None, "ctx", "tp"),
        P(None, None, "tp"),
        P(None, "tp"),
        P("tp"),
    )
    out_specs = (P(("ctx", "tp"), None), P("ctx", "tp"))
    return jax.shard_map(body, mesh=mesh, in_specs=in_specs, out_specs=out_specs, check_vma=False)
```
